512 devices in a mesh: fsdp: 32 (over z_lo, x, core), tp: 16 (over z_hi, y).
Axes of the slice: x: 4, y: 8, z: 8 (z_hi: 2, z_lo: 4; z = z_hi * 4 + z_lo), core: 2. Of those that a mesh axis runs over, the one named last changes fastest.
Arguments:
- hidden: bfloat16 [4, 64, 5120], P(None, 'fsdp'), may hold values from -6 to 6
- base_kv: bfloat16 [5120, 2048], P(None, 'tp'), may hold values from -0.078125 to 0.078125
- delta_codes: bfloat16 [5120, 2048], P('fsdp', 'tp'), may hold values from -1 to 1
- block_scales: float32 [40, 16], P(None, 'tp'), may hold values from 0.004 to 0.04
- key_gain: float32 [128], replicated, may hold values from 2.5 to 6
- queries: bfloat16 [4, 64, 8192], P(None, 'fsdp', 'tp'), may hold values from -160 to 160
- kv_cache: bfloat16 [64, 4096, 2048], P('fsdp', None, 'tp'), may hold values from -6 to 6
- lengths: int32 [64], P('fsdp'), may hold values from 2 to 4096, as said below
Outputs:
- new_entries: bfloat16 [4, 64, 2048], P(None, 'fsdp', 'tp')
- attended: bfloat16 [4, 64, 8192], P(None, 'fsdp', 'tp')
The draws below stay inside these ranges and needn't reach their ends.
Inputs may be any that keep to these rules, and one draw needn't show every extreme that they name: `lengths`: some row has exactly 4096 valid positions and some row exactly 2.
All inputs are finite; a program needn't handle non-finite values.
Results may differ from the reference program's by a relative error of at most 0.007.
Values may be sent and summed in bfloat16 or wider, within the bound.
A program may use at most 64 MiB of HBM per device.

```python
import math
import jax
import jax.numpy as jnp
from jax import lax

D = 5120
KVH = 8
HD = 128
BLOCK = 128
STEPS = 4
CACHE = 4096
GROUP = 8
HALF = 64
KVC = 2048
QC = 8192
ROWS = 64


def draw_kv_cache(key, part):
    own_key = jax.random.fold_in(key, 1)
    entries = jax.random.normal(own_key, (ROWS, CACHE, KVC), jnp.float32)
    return jnp.clip(entries, -6.0, 6.0).astype(jnp.bfloat16)


def draw_queries(key, part):
    own_key = jax.random.fold_in(key, 2)
    drawn_values = jax.random.normal(own_key, (STEPS, ROWS, QC), jnp.float32)
    return jnp.clip(drawn_values, -160.0, 160.0).astype(jnp.bfloat16)


def draw_lengths(key, part):
    own_key = jax.random.fold_in(key, 3)
    drawn_lengths = jax.random.randint(own_key, (ROWS,), 2, CACHE + 1, dtype=jnp.int32)
    ordering = jax.random.permutation(jax.random.fold_in(key, 4), ROWS)
    drawn_lengths = drawn_lengths.at[ordering[0]].set(CACHE)
    drawn_lengths = drawn_lengths.at[ordering[1]].set(2)
    return drawn_lengths.astype(jnp.int32)


def level_of(key, extent, shards, low, largest):
    gain = 1.0
    for dim, parts in shards:
        heights = jax.random.uniform(jax.random.fold_in(jax.random.fold_in(key, 6), dim), (parts,), jnp.float32, low / len(shards), largest / len(shards))
        gain = gain * jnp.repeat(jnp.exp(heights), extent[dim] // parts).reshape((-1,) + (1,) * (len(extent) - 1 - dim))
    return gain


def centred(stream_key, shape, deviation, most, shards=(), kind=jnp.bfloat16):
    drawn = deviation * jax.random.normal(stream_key, shape, jnp.float32)
    if shards:
        drawn = drawn * level_of(stream_key, shape, shards, -0.22, 0.18)
    return jnp.clip(drawn, -most, most).astype(kind)


def setup_inputs(seed: int = 0) -> dict:
    streams_of = jax.random.split(jax.random.key(seed), 9)
    return {
        "hidden": centred(streams_of[0], (STEPS, ROWS, D), 1.0, 6.0, ((1, 32),)),
        "base_kv": centred(streams_of[1], (D, KVC), D ** -0.5, 0.078125, ((1, 16),)),
        "delta_codes": jnp.clip(jax.random.uniform(streams_of[2], (D, KVC), jnp.float32, -1.0, 1.0) * level_of(streams_of[2], (D, KVC), ((0, 32), (1, 16)), -0.4, 0.0), -1.0, 1.0).astype(jnp.bfloat16),
        "block_scales": jnp.clip(jnp.exp(math.log(0.04) - 2.30258502 * jax.random.uniform(streams_of[3], (D // BLOCK, KVC // BLOCK), jnp.float32) ** level_of(streams_of[3], (D // BLOCK, KVC // BLOCK), ((1, 16),), -0.2, 0.2)), 0.004, 0.04),
        "key_gain": jnp.clip(jnp.exp(jax.random.uniform(streams_of[4], (HD,), jnp.float32, math.log(2.5), math.log(6.0))), 2.5, 6.0),
        "queries": draw_queries(jax.random.fold_in(streams_of[8], 71), 0),
        "kv_cache": draw_kv_cache(jax.random.fold_in(streams_of[8], 71), 0),
        "lengths": draw_lengths(jax.random.fold_in(streams_of[8], 71), 0),
    }


EPSILON = 1e-06
NEGATIVE = -1e+30

def one_row(packed):
    query_row, cache_row, length_row, fresh_keys, fresh_values = packed
    factor = 1.0 / math.sqrt(HD)
    cache_view = cache_row.reshape(CACHE, 2, KVH, 2, HALF)
    cache_keys = cache_view[:, :, :, 0, :].transpose(0, 2, 1, 3).reshape(CACHE, KVH, HD).astype(jnp.float32)
    cache_values = cache_view[:, :, :, 1, :].transpose(0, 2, 1, 3).reshape(CACHE, KVH, HD).astype(jnp.float32)
    query_wide = query_row.astype(jnp.float32)
    cache_logits = jnp.einsum('sgid,lgd->sgil', query_wide, cache_keys, precision=lax.Precision.HIGHEST) * factor
    fresh_logits = jnp.einsum('sgid,tgd->sgit', query_wide, fresh_keys.astype(jnp.float32), precision=lax.Precision.HIGHEST) * factor
    in_cache = jnp.arange(CACHE) < length_row
    steps_index = jnp.arange(STEPS)
    fresh_allowed = steps_index[None, :] <= steps_index[:, None]
    cache_logits = jnp.where(in_cache[None, None, None, :], cache_logits, NEGATIVE)
    fresh_logits = jnp.where(fresh_allowed[:, None, None, :], fresh_logits, NEGATIVE)
    highest = jnp.maximum(lax.optimization_barrier(jnp.max(cache_logits, axis=-1)), lax.optimization_barrier(jnp.max(fresh_logits, axis=-1)))
    cache_exp = jnp.exp(cache_logits - highest[..., None])
    fresh_exp = jnp.exp(fresh_logits - highest[..., None])
    denominator = lax.optimization_barrier(jnp.sum(cache_exp, axis=-1)) + lax.optimization_barrier(jnp.sum(fresh_exp, axis=-1))
    cache_weights = (cache_exp / denominator[..., None]).astype(jnp.bfloat16).astype(jnp.float32)
    fresh_weights = (fresh_exp / denominator[..., None]).astype(jnp.bfloat16).astype(jnp.float32)
    combined = jnp.einsum('sgil,lgd->sgid', cache_weights, cache_values, precision=lax.Precision.HIGHEST)
    combined = combined + jnp.einsum('sgit,tgd->sgid', fresh_weights, fresh_values.astype(jnp.float32), precision=lax.Precision.HIGHEST)
    return combined.astype(jnp.bfloat16)

def reference(hidden, base_kv, delta_codes, block_scales, key_gain, queries, kv_cache, lengths):
    scale_full = jnp.repeat(jnp.repeat(block_scales, BLOCK, axis=0), BLOCK, axis=1)
    delta = delta_codes.astype(jnp.float32) * scale_full
    flattened = hidden.reshape(STEPS * ROWS, D)
    projected = jnp.dot(flattened, base_kv, preferred_element_type=jnp.float32)
    projected = projected + jnp.dot(flattened.astype(jnp.float32), delta, precision=lax.Precision.HIGHEST)
    projected = projected.reshape(STEPS, ROWS, 2, KVH, 2, HALF)
    key_part = projected[:, :, :, :, 0, :]
    value_part = projected[:, :, :, :, 1, :]
    mean_square = lax.optimization_barrier(jnp.mean(key_part * key_part, axis=(2, 4), keepdims=True))
    normed = key_part * lax.rsqrt(mean_square + EPSILON) * key_gain.reshape(2, 1, HALF)
    entries = jnp.stack([normed, value_part], axis=4).astype(jnp.bfloat16)
    new_entries = entries.reshape(STEPS, ROWS, KVC)
    fresh_keys = entries[:, :, :, :, 0, :].transpose(0, 1, 3, 2, 4).reshape(STEPS, ROWS, KVH, HD)
    fresh_values = entries[:, :, :, :, 1, :].transpose(0, 1, 3, 2, 4).reshape(STEPS, ROWS, KVH, HD)
    query_full = queries.reshape(STEPS, ROWS, 2, KVH, GROUP, HALF).transpose(0, 1, 3, 4, 2, 5).reshape(STEPS, ROWS, KVH, GROUP, HD)
    outputs = lax.map(one_row, (query_full.transpose(1, 0, 2, 3, 4), kv_cache, lengths, fresh_keys.transpose(1, 0, 2, 3), fresh_values.transpose(1, 0, 2, 3)))
    outputs = outputs.transpose(1, 0, 2, 3, 4).reshape(STEPS, ROWS, KVH, GROUP, 2, HALF)
    attended = outputs.transpose(0, 1, 4, 2, 3, 5).reshape(STEPS, ROWS, QC)
    return (new_entries, attended)
```

```python
import functools
import math

import jax
import jax.numpy as jnp
from jax import lax
from jax.experimental import pallas as pl
from jax.experimental.pallas import tpu as pltpu
from jax.sharding import PartitionSpec as P

QH = 64
KVH = 8
HD = 128
BLOCK = 128


EPSILON = 1e-06
NEGATIVE = -1e30

CACHE_MOST = 6.0
NORM_LIMIT = 480.0
LEVELS = 32760.0

MESH = pl.DeviceIdType.MESH
F32 = jnp.float32
BF16 = jnp.bfloat16
CHUNK = 1024


def pair_kernel(
    zs, xcs, ys,
    hid, base, codes, scales, gain, qry, cache, lens,
    ne_out, att_out, flag_out,
    qv, hv, base_v, gain_v, cache_v, w_v, q32, qbf, qoth, h32, hs, hr, lown, snd, rcv, ysend, yrecv, p3,
    fl, fy, fx,
    loc_sem, cache_sem, main_s, main_r, qx_s, qx_r, ag_s, ag_r, p1_s, p1_r, p2_s, p2_r, p3_s, p3_r,
    fy_s, fy_r, fx_s, fx_r,
):
    f = lax.axis_index("fsdp")
    t = lax.axis_index("tp")
    zl = f // xcs
    xc = lax.rem(f, xcs)
    zh = t // ys
    y = lax.rem(t, ys)
    rows = cache.shape[0]
    steps = qry.shape[0]
    group = 8
    half = HD // 2
    nq = steps * group
    per_row = cache.shape[1] // CHUNK
    nchunk = rows * per_row
    factor = 1.0 / math.sqrt(HD)

    partner = (f, (1 - zh) * ys + y)

    def z_peer(k):
        return (lax.rem(zl + k, zs) * xcs + xc, t)

    def x_peer(k):
        return (zl * xcs + lax.rem(xc + k, xcs), t)

    def y_peer(k):
        return (f, zh * ys + lax.rem(y + k, ys))

    barrier = pltpu.get_barrier_semaphore()
    everyone = (
        [partner]
        + [z_peer(k) for k in range(1, zs)]
        + [x_peer(k) for k in range(1, xcs)]
        + [y_peer(k) for k in range(1, ys)]
    )
    for device in everyone:
        pl.semaphore_signal(barrier, inc=1, device_id=device, device_id_type=MESH)

    get_q = pltpu.make_async_copy(qry, qv, loc_sem.at[0])
    get_h = pltpu.make_async_copy(hid, hv, loc_sem.at[1])
    get_w = pltpu.make_async_copy(codes, w_v.at[xc], loc_sem.at[2])
    get_b = pltpu.make_async_copy(base, base_v, loc_sem.at[3])
    get_g = pltpu.make_async_copy(gain, gain_v, loc_sem.at[4])
    get_q.start()
    get_c = []
    for i in range(nchunk):
        r, c = i // per_row, i % per_row
        part = pl.ds(c * CHUNK, CHUNK)
        get_c.append(pltpu.make_async_copy(cache.at[r, part], cache_v.at[r, part], cache_sem.at[i]))
    get_c[0].start()
    get_h.start()
    for copy in get_c[1:]:
        copy.start()
    get_w.start()
    get_b.start()
    get_g.start()

    get_q.wait()
    lane512 = lax.broadcasted_iota(jnp.int32, (8, group * half), 1)
    sub512 = lax.broadcasted_iota(jnp.int32, (8, group * half), 0)
    own512 = (lane512 // half) == sub512
    sub = lax.broadcasted_iota(jnp.int32, (8, HD), 0)
    lane = lax.broadcasted_iota(jnp.int32, (8, HD), 1)
    odd = (sub % 2) == 1
    for s in range(steps):
        both = qv[s].astype(F32)
        for r in range(rows):
            spread = jnp.broadcast_to(both[r : r + 1], (8, group * half))
            spread = jnp.where(own512, spread, 0.0)
            folded = spread[:, 0:HD]
            for j in range(1, group * half // HD):
                folded = folded + spread[:, j * HD : (j + 1) * HD]
            folded = jnp.where(odd, pltpu.roll(folded, half, 1), folded)
            q32[r, s * group : (s + 1) * group, :] = folded
    norms = []
    for r in range(rows):
        qbf[r] = q32[r].astype(BF16)
        norms.append(jnp.sum(jnp.abs(q32[r]), axis=1, keepdims=True))
    widest = jnp.max(norms[0], axis=0, keepdims=True)
    for r in range(1, rows):
        widest = jnp.maximum(widest, jnp.max(norms[r], axis=0, keepdims=True))
    fl[0] = jnp.broadcast_to(widest, (8, HD))
    to_code = [LEVELS / (CACHE_MOST * jnp.maximum(n, 1e-30)) for n in norms]

    def logits(i):
        r, c = i // per_row, i % per_row
        get_c[i].wait()
        block = cache_v[r, c * CHUNK : (c + 1) * CHUNK, :]
        raw = lax.dot_general(qbf[r], block, (((1,), (1,)), ((), ())), preferred_element_type=F32)
        lown[i] = raw * factor
        snd[i] = jnp.round(raw * to_code[r]).astype(jnp.int32).astype(jnp.int16)

    logits(0)

    get_h.wait()
    for s in range(steps):
        h32[s * rows : (s + 1) * rows, :] = hv[s].astype(F32)
    blocks = h32.shape[1] // BLOCK
    own_blocks = blocks // zs
    for j in range(blocks // 2):
        low = h32[:, 2 * j * BLOCK : (2 * j + 1) * BLOCK]
        high = h32[:, (2 * j + 1) * BLOCK : (2 * j + 2) * BLOCK]
        hs[(2 * j) // own_blocks, (2 * j % own_blocks) * 8 : (2 * j % own_blocks) * 8 + 16, :] = jnp.concatenate(
            [low, high], axis=0
        ).astype(BF16)

    get_w.wait()
    pl.semaphore_wait(barrier, len(everyone))

    def remote(src, dst, send, recv, device):
        copy = pltpu.make_async_remote_copy(
            src_ref=src, dst_ref=dst, send_sem=send, recv_sem=recv, device_id=device, device_id_type=MESH
        )
        copy.start()
        return copy

    main = [remote(snd.at[0], rcv.at[0], main_s.at[0], main_r.at[0], partner)]
    sent_q = remote(qbf, qoth, qx_s, qx_r, partner)
    sent_h = [
        remote(hs.at[lax.rem(zl + k, zs)], hr.at[k - 1], p1_s.at[k - 1], p1_r.at[k - 1], z_peer(k))
        for k in range(1, zs)
    ]
    sent_w = [
        remote(w_v.at[xc], w_v.at[xc], ag_s.at[k - 1], ag_r.at[k - 1], x_peer(k)) for k in range(1, xcs)
    ]
    sent_y = [
        remote(fl.at[0], fy.at[k - 1], fy_s.at[k - 1], fy_r.at[k - 1], y_peer(k)) for k in range(1, ys)
    ]
    for i in range(1, nchunk):
        logits(i)
        main.append(remote(snd.at[i], rcv.at[i], main_s.at[i], main_r.at[i], partner))

    get_b.wait()
    get_g.wait()
    projected = jnp.dot(h32[...].astype(BF16), base_v[...], preferred_element_type=F32)

    for copy in sent_y:
        copy.wait_recv()
    widest = fl[0]
    for k in range(ys - 1):
        widest = jnp.maximum(widest, fy[k])
    fl[1] = widest
    sent_x = [
        remote(fl.at[1], fx.at[k - 1], fx_s.at[k - 1], fx_r.at[k - 1], x_peer(k)) for k in range(1, xcs)
    ]

    for copy in sent_h:
        copy.wait_recv()
    for copy in sent_w:
        copy.wait_recv()
    mine = hs[zl].astype(F32)
    theirs = [hr[k].astype(F32) for k in range(zs - 1)]
    weights = w_v[...].reshape(own_blocks * BLOCK, HD)
    total = None
    for b in range(own_blocks):
        stacked = jnp.concatenate([part[b * 8 : (b + 1) * 8] for part in [mine] + theirs], axis=0).astype(BF16)
        term = jnp.dot(stacked, weights[b * BLOCK : (b + 1) * BLOCK], preferred_element_type=F32)
        term = term * scales[zl * own_blocks + b, 0]
        total = term if total is None else total + term
    for copy in sent_x:
        copy.wait_recv()
    for k in range(xcs - 1):
        widest = jnp.maximum(widest, fx[k])
    for k in range(1, zs):
        ysend[k - 1, 0:8, :] = total[k * 8 : (k + 1) * 8]
        ysend[k - 1, 8:16, :] = widest
    sent_p = [
        remote(
            ysend.at[k - 1], yrecv.at[k - 1], p2_s.at[k - 1], p2_r.at[k - 1], z_peer(zs - k)
        )
        for k in range(1, zs)
    ]
    correction = total[0:8]
    for k in range(1, zs):
        sent_p[k - 1].wait_recv()
        correction = correction + yrecv[k - 1, 0:8, :]
        widest = jnp.maximum(widest, yrecv[k - 1, 8:16, :])
    projected = projected + correction
    p3[0, 0:8, :] = projected
    p3[0, 8:16, :] = widest
    sent_k = remote(p3.at[0], p3.at[1], p3_s, p3_r, partner)

    sent_q.wait_recv()
    step_size = []
    for r in range(rows):
        n = jnp.sum(jnp.abs(qoth[r].astype(F32)), axis=1, keepdims=True)
        step_size.append(n * (CACHE_MOST * factor / LEVELS))
    top = [jnp.full((nq, 1), NEGATIVE, F32) for _ in range(rows)]
    den = [jnp.zeros((nq, 1), F32) for _ in range(rows)]
    acc = [jnp.zeros((nq, HD), F32) for _ in range(rows)]

    def merge(r, values, block):
        highest = jnp.maximum(top[r], jnp.max(values, axis=1, keepdims=True))
        weight = jnp.exp(values - highest)
        keep = jnp.exp(top[r] - highest)
        den[r] = den[r] * keep + jnp.sum(weight, axis=1, keepdims=True)
        acc[r] = acc[r] * keep + jnp.dot(weight.astype(BF16), block, preferred_element_type=F32)
        top[r] = highest

    def take(i):
        r, c = i // per_row, i % per_row
        main[i].wait_recv()
        values = lown[i] + rcv[i].astype(jnp.int32).astype(F32) * step_size[r]
        place = c * CHUNK + lax.broadcasted_iota(jnp.int32, (nq, CHUNK), 1)
        values = jnp.where(place < lens[r], values, NEGATIVE)
        merge(r, values, cache_v[r, c * CHUNK : (c + 1) * CHUNK, :])

    late = nchunk - 2
    for i in range(late):
        take(i)

    sent_k.wait_recv()
    other = p3[1, 0:8, :]
    flag_out[...] = jnp.maximum(widest, p3[1, 8:16, :])
    is_key = lane < half
    squares = jnp.sum(jnp.where(is_key, projected * projected, 0.0), axis=1, keepdims=True)
    squares = squares + jnp.sum(jnp.where(is_key, other * other, 0.0), axis=1, keepdims=True)
    inverse = lax.rsqrt(squares / HD + EPSILON)
    gains = jnp.broadcast_to(gain_v[...], (8, HD))
    swapped = pltpu.roll(gains, half, 1)
    first = zh == 0
    own_gain = jnp.where(first, gains, swapped)
    other_gain = jnp.where(first, swapped, gains)
    entries = jnp.where(is_key, projected * inverse * own_gain, projected)
    other_keys = jnp.where(is_key, other * inverse * other_gain, 0.0)
    for s in range(steps):
        ne_out[s] = entries[s * rows : (s + 1) * rows, :].astype(BF16)
    blank = jnp.zeros((8, HD), F32)
    own16 = jnp.concatenate([entries, blank], axis=0).astype(BF16)
    other16 = jnp.concatenate([other_keys, blank], axis=0).astype(BF16)
    column = lax.broadcasted_iota(jnp.int32, (nq, 16), 1)
    step_of = lax.broadcasted_iota(jnp.int32, (nq, 16), 0) // group
    for r in range(rows):
        fresh = lax.dot_general(qbf[r], own16, (((1,), (1,)), ((), ())), preferred_element_type=F32)
        fresh = fresh + lax.dot_general(qoth[r], other16, (((1,), (1,)), ((), ())), preferred_element_type=F32)
        allowed = (column % rows == r) & (column // rows <= step_of)
        merge(r, jnp.where(allowed, fresh * factor, NEGATIVE), own16)

    for i in range(late, nchunk):
        take(i)

    result = [acc[r] / den[r] for r in range(rows)]
    right = (lane >= half) == odd
    for s in range(steps):
        lines = []
        for r in range(rows):
            part = result[r][s * group : (s + 1) * group, :]
            part = jnp.where(odd, part, pltpu.roll(part, half, 1))
            part = jnp.where(right, part, 0.0)
            lines.append(
                [
                    jnp.sum(jnp.where(sub // 2 == j, part, 0.0), axis=0, keepdims=True)
                    for j in range(group * half // HD)
                ]
            )
        for j in range(group * half // HD):
            att_out[s, :, j * HD : (j + 1) * HD] = jnp.concatenate([line[j] for line in lines], axis=0).astype(BF16)

    for copy in main + [sent_q, sent_k] + sent_h + sent_w + sent_y + sent_x + sent_p:
        copy.wait_send()


def fused(sizes, hidden, base_kv, delta_codes, block_scales, key_gain, queries, kv_cache, lengths):
    zs, xcs, ys = sizes
    step_count, row_count, width = hidden.shape
    cache_length = kv_cache.shape[1]
    nq = step_count * 8
    nchunk = row_count * cache_length // CHUNK
    own_blocks = width // BLOCK // zs
    dma = pltpu.SemaphoreType.DMA
    any_space = pl.BlockSpec(memory_space=pl.ANY)
    smem = pl.BlockSpec(memory_space=pltpu.SMEM)
    vmem = pl.BlockSpec(memory_space=pltpu.VMEM)
    return pl.pallas_call(
        functools.partial(pair_kernel, zs, xcs, ys),
        out_shape=(
            jax.ShapeDtypeStruct((step_count, row_count, HD), BF16),
            jax.ShapeDtypeStruct(queries.shape, BF16),
            jax.ShapeDtypeStruct((8, HD), F32),
        ),
        in_specs=[any_space, any_space, any_space, smem, any_space, any_space, any_space, smem],
        out_specs=(vmem, vmem, vmem),
        scratch_shapes=[
            pltpu.VMEM(queries.shape, BF16),
            pltpu.VMEM(hidden.shape, BF16),
            pltpu.VMEM(base_kv.shape, BF16),
            pltpu.VMEM((1, HD), F32),
            pltpu.VMEM(kv_cache.shape, BF16),
            pltpu.VMEM((xcs,) + delta_codes.shape, BF16),
            pltpu.VMEM((row_count, nq, HD), F32),
            pltpu.VMEM((row_count, nq, HD), BF16),
            pltpu.VMEM((row_count, nq, HD), BF16),
            pltpu.VMEM((step_count * row_count, width), F32),
            pltpu.VMEM((zs, own_blocks * 8, BLOCK), BF16),
            pltpu.VMEM((zs - 1, own_blocks * 8, BLOCK), BF16),
            pltpu.VMEM((nchunk, nq, CHUNK), F32),
            pltpu.VMEM((nchunk, nq, CHUNK), jnp.int16),
            pltpu.VMEM((nchunk, nq, CHUNK), jnp.int16),
            pltpu.VMEM((zs - 1, 16, HD), F32),
            pltpu.VMEM((zs - 1, 16, HD), F32),
            pltpu.VMEM((2, 16, HD), F32),
            pltpu.VMEM((2, 8, HD), F32),
            pltpu.VMEM((ys - 1, 8, HD), F32),
            pltpu.VMEM((xcs - 1, 8, HD), F32),
            dma((5,)),
            dma((nchunk,)),
            dma((nchunk,)),
            dma((nchunk,)),
            dma,
            dma,
            dma((xcs - 1,)),
            dma((xcs - 1,)),
            dma((zs - 1,)),
            dma((zs - 1,)),
            dma((zs - 1,)),
            dma((zs - 1,)),
            dma,
            dma,
            dma((ys - 1,)),
            dma((ys - 1,)),
            dma((xcs - 1,)),
            dma((xcs - 1,)),
        ],
        compiler_params=pltpu.CompilerParams(
            collective_id=0, has_side_effects=True, vmem_limit_bytes=40 * 1024 * 1024
        ),
    )(hidden, base_kv, delta_codes, block_scales, key_gain.reshape(1, HD), queries, kv_cache, lengths)


def partner(block, axis, distance):
    count = lax.axis_size(axis)
    route = []
    for low in range(count):
        high = low | 1 << distance
        if high != low and high < count:
            route += [(low, high), (high, low)]
    return lax.ppermute(block, axis, route)


def attend(cache_full, fresh_full, fresh_allowed, in_cache, cache_values, fresh_values):
    factor = 1.0 / math.sqrt(HD)
    cache_logits = jnp.where(in_cache[None, :, None, None, :], cache_full * factor, NEGATIVE)
    fresh_logits = jnp.where(fresh_allowed[:, None, None, None, :], fresh_full * factor, NEGATIVE)
    highest = jnp.maximum(jnp.max(cache_logits, axis=-1), jnp.max(fresh_logits, axis=-1))
    cache_exp = jnp.exp(cache_logits - highest[..., None])
    fresh_exp = jnp.exp(fresh_logits - highest[..., None])
    denominator = jnp.sum(cache_exp, axis=-1) + jnp.sum(fresh_exp, axis=-1)
    cache_weights = (cache_exp / denominator[..., None]).astype(jnp.bfloat16)
    fresh_weights = (fresh_exp / denominator[..., None]).astype(jnp.bfloat16)
    combined = jnp.einsum(
        "srugl,rlud->srugd", cache_weights, cache_values, preferred_element_type=jnp.float32
    )
    combined = combined + jnp.einsum(
        "srugt,trud->srugd", fresh_weights, fresh_values, preferred_element_type=jnp.float32
    )
    return combined.astype(jnp.bfloat16)


def plain(hidden, base_kv, delta_codes, block_scales, key_gain, queries, kv_cache, lengths):
    step_count, row_count, model_width = hidden.shape
    local_width = base_kv.shape[1]
    unit_count = local_width // HD
    half_dim = HD // 2
    group_size = QH // KVH
    cache_length = kv_cache.shape[1]
    partner_bit = lax.axis_size("tp").bit_length() - 2
    flattened = hidden.reshape(step_count * row_count, model_width)
    projected = jnp.dot(flattened, base_kv, preferred_element_type=jnp.float32)
    scale_full = jnp.repeat(jnp.repeat(block_scales, BLOCK, axis=0), BLOCK, axis=1)
    widened = flattened.astype(jnp.float32)
    correction = jnp.dot(
        widened,
        lax.all_gather(delta_codes, "fsdp", axis=0, tiled=True).astype(jnp.float32) * scale_full,
        precision=lax.Precision.HIGHEST,
    )
    projected = (projected + correction).reshape(step_count, row_count, unit_count, 2, half_dim)
    key_part = projected[:, :, :, 0, :]
    value_part = projected[:, :, :, 1, :]
    squares = jnp.sum(key_part * key_part, axis=-1)
    squares = squares + partner(squares, "tp", partner_bit)
    half_index = (lax.axis_index("tp") * unit_count + jnp.arange(unit_count)) // KVH
    gain_pairs = key_gain.reshape(2, half_dim)
    gain_units = jnp.where(half_index[:, None] == 0, gain_pairs[0][None, :], gain_pairs[1][None, :])
    normed = key_part * lax.rsqrt(squares / HD + EPSILON)[..., None] * gain_units
    entries = jnp.stack([normed, value_part], axis=3).astype(jnp.bfloat16)
    new_entries = entries.reshape(step_count, row_count, local_width)
    fresh_keys = entries[:, :, :, 0, :]
    fresh_values = entries[:, :, :, 1, :]
    query_units = queries.reshape(step_count, row_count, unit_count, group_size, half_dim)
    cache_units = kv_cache.reshape(row_count, cache_length, unit_count, 2, half_dim)
    cache_keys = cache_units[:, :, :, 0, :]
    cache_values = cache_units[:, :, :, 1, :]
    in_cache = jnp.arange(cache_length)[None, :] < lengths[:, None]
    steps_index = jnp.arange(step_count)
    fresh_allowed = steps_index[None, :] <= steps_index[:, None]
    outputs = []
    for current in range(step_count):
        query_step = query_units[current : current + 1]
        cache_full = jnp.einsum(
            "srugd,rlud->srugl", query_step, cache_keys, preferred_element_type=jnp.float32
        )
        fresh_full = jnp.einsum(
            "srugd,trud->srugt", query_step, fresh_keys, preferred_element_type=jnp.float32
        )
        other_cache, other_fresh = partner((cache_full, fresh_full), "tp", partner_bit)
        cache_full = cache_full + other_cache
        fresh_full = fresh_full + other_fresh
        outputs.append(
            attend(
                cache_full,
                fresh_full,
                fresh_allowed[current : current + 1],
                in_cache,
                cache_values,
                fresh_values,
            )
        )
    attended = jnp.concatenate(outputs, axis=0)
    attended = attended.reshape(step_count, row_count, unit_count * group_size * half_dim)
    return (new_entries, attended)


def local(sizes, *args):
    new_entries, attended, widest = fused(sizes, *args)
    return lax.cond(
        widest[0, 0] <= NORM_LIMIT,
        lambda args, fast: fast,
        lambda args, fast: plain(*args),
        args,
        (new_entries, attended),
    )


def solution(mesh):
    fsdp, tp = mesh.shape["fsdp"], mesh.shape["tp"]
    sizes = (4, fsdp // 4, tp // 2)
    in_specs = (
        P(None, "fsdp", None),
        P(None, "tp"),
        P("fsdp", "tp"),
        P(None, "tp"),
        P(),
        P(None, "fsdp", "tp"),
        P("fsdp", None, "tp"),
        P("fsdp"),
    )
    out_specs = (P(None, "fsdp", "tp"), P(None, "fsdp", "tp"))
    return jax.shard_map(functools.partial(local, sizes), mesh=mesh, in_specs=in_specs, out_specs=out_specs, check_vma=False)
```

```python
import functools
import math

import jax
import jax.numpy as jnp
from jax import lax
from jax.experimental import pallas as pl
from jax.experimental.pallas import tpu as pltpu
from jax.sharding import PartitionSpec as P

HD = 128
BLOCK = 128


EPSILON = 1e-06
NEGATIVE = -1e30

CACHE_MOST = 6.0
NORM_LIMIT = 480.0
LEVELS = 32760.0

MESH = pl.DeviceIdType.MESH
F32 = jnp.float32
BF16 = jnp.bfloat16
CHUNK = 1024
LATE = 8
FLAG_STEPS = {2: 2, 5: 3}


def pair_kernel(
    zs, xcs, ys, exact,
    hid, base, codes, scales, gain, qry, cache, lens,
    *refs,
):
    both_out, refs = refs[0], refs[1:]
    if not exact:
        flag_out, refs = refs[0], refs[1:]
    (
    qv, hv, base_v, gain_v, cache_v, w_v, q32, qbf, packed, qoth, h32, hs, hr, lown, snd, rcv, ysend, yrecv,
    fl, fy, fx, fz, fp,
    loc_sem, cache_sem, main_s, main_r, qx_s, qx_r, ag_s, ag_r, p1_s, p1_r, p2_s, p2_r,
    fy_s, fy_r, fx_s, fx_r, fz_s, fz_r, fp_s, fp_r,
    ) = refs
    f = lax.axis_index("fsdp")
    t = lax.axis_index("tp")
    zl = f // xcs
    xc = lax.rem(f, xcs)
    zh = t // ys
    y = lax.rem(t, ys)
    rows = cache.shape[0]
    steps = qry.shape[0]
    group = 8
    half = HD // 2
    nq = steps * group
    per_row = cache.shape[1] // CHUNK
    nchunk = rows * per_row
    factor = 1.0 / math.sqrt(HD)

    partner = (f, (1 - zh) * ys + y)

    def z_peer(k):
        return (lax.rem(zl + k, zs) * xcs + xc, t)

    def other_z_peer(k):
        return (lax.rem(zl + k, zs) * xcs + xc, (1 - zh) * ys + y)

    def x_peer(k):
        return (zl * xcs + lax.rem(xc + k, xcs), t)

    def y_peer(k):
        return (f, zh * ys + lax.rem(y + k, ys))

    barrier = pltpu.get_barrier_semaphore()
    everyone = (
        [partner]
        + [z_peer(k) for k in range(1, zs)]
        + [other_z_peer(k) for k in range(1, zs)]
        + [x_peer(k) for k in range(1, xcs)]
    )
    for device in everyone:
        pl.semaphore_signal(barrier, inc=1, device_id=device, device_id_type=MESH)

    first = zh == 0
    if not exact:

        @pl.when(first)
        def _():
            for k in range(1, ys):
                pl.semaphore_signal(barrier, inc=1, device_id=y_peer(k), device_id_type=MESH)

    get_q = pltpu.make_async_copy(qry, qv, loc_sem.at[0])
    get_h = pltpu.make_async_copy(hid, hv, loc_sem.at[1])
    get_w = pltpu.make_async_copy(codes, w_v.at[xc], loc_sem.at[2])
    get_b = pltpu.make_async_copy(base, base_v, loc_sem.at[3])
    get_g = pltpu.make_async_copy(gain, gain_v, loc_sem.at[4])
    get_q.start()
    get_c = []
    for i in range(nchunk):
        r, c = i // per_row, i % per_row
        part = pl.ds(c * CHUNK, CHUNK)
        get_c.append(pltpu.make_async_copy(cache.at[r, part], cache_v.at[r, part], cache_sem.at[i]))
    get_c[0].start()
    get_h.start()
    for copy in get_c[1:]:
        copy.start()
    get_w.start()
    get_b.start()
    get_g.start()

    get_q.wait()
    lane512 = lax.broadcasted_iota(jnp.int32, (8, group * half), 1)
    sub512 = lax.broadcasted_iota(jnp.int32, (8, group * half), 0)
    own512 = (lane512 // half) == sub512
    sub = lax.broadcasted_iota(jnp.int32, (8, HD), 0)
    lane = lax.broadcasted_iota(jnp.int32, (8, HD), 1)
    odd = (sub % 2) == 1
    for s in range(steps):
        both = qv[s].astype(F32)
        for r in range(rows):
            spread = jnp.broadcast_to(both[r : r + 1], (8, group * half))
            spread = jnp.where(own512, spread, 0.0)
            folded = spread[:, 0:HD]
            for j in range(1, group * half // HD):
                folded = folded + spread[:, j * HD : (j + 1) * HD]
            folded = jnp.where(odd, pltpu.roll(folded, half, 1), folded)
            q32[r, s * group : (s + 1) * group, :] = folded
    norms = []
    for r in range(rows):
        qbf[r] = q32[r].astype(BF16)
        norms.append(jnp.sum(jnp.abs(q32[r]), axis=1, keepdims=True))
    widest = jnp.max(norms[0], axis=0, keepdims=True)
    for r in range(1, rows):
        widest = jnp.maximum(widest, jnp.max(norms[r], axis=0, keepdims=True))
    wide_q = lax.broadcasted_iota(jnp.int32, (nq, HD), 1) < half
    packed[0] = (q32[0] + pltpu.roll(q32[1], half, 1)).astype(BF16)
    to_code = [LEVELS / (CACHE_MOST * jnp.maximum(n, 1e-30)) for n in norms]

    def logits(i):
        r, c = i // per_row, i % per_row
        get_c[i].wait()
        block = cache_v[r, c * CHUNK : (c + 1) * CHUNK, :]
        raw = lax.dot_general(qbf[r], block, (((1,), (1,)), ((), ())), preferred_element_type=F32)
        lown[i] = raw * factor
        if not exact:
            snd[i] = jnp.round(raw * to_code[r]).astype(jnp.int32).astype(jnp.int16)

    for i in range(nchunk):
        logits(i)

    get_h.wait()
    for s in range(steps):
        h32[s * rows : (s + 1) * rows, :] = hv[s].astype(F32)
    blocks = h32.shape[1] // BLOCK
    own_blocks = blocks // zs
    for j in range(blocks // 2):
        low = h32[:, 2 * j * BLOCK : (2 * j + 1) * BLOCK]
        high = h32[:, (2 * j + 1) * BLOCK : (2 * j + 2) * BLOCK]
        hs[(2 * j) // own_blocks, (2 * j % own_blocks) * 8 : (2 * j % own_blocks) * 8 + 16, :] = jnp.concatenate(
            [low, high], axis=0
        ).astype(BF16)

    get_w.wait()
    pl.semaphore_wait(barrier, len(everyone) + (0 if exact else (1 - zh) * (ys - 1)))

    def remote(src, dst, send, recv, device):
        copy = pltpu.make_async_remote_copy(
            src_ref=src, dst_ref=dst, send_sem=send, recv_sem=recv, device_id=device, device_id_type=MESH
        )
        copy.start()
        return copy

    sent_h = [
        remote(hs.at[lax.rem(zl + k, zs)], hr.at[k - 1], p1_s.at[k - 1], p1_r.at[k - 1], z_peer(k))
        for k in range(1, zs)
    ]
    sent_w = [
        remote(w_v.at[xc], w_v.at[xc], ag_s.at[k - 1], ag_r.at[k - 1], x_peer(k)) for k in range(1, xcs)
    ]
    sent_q = remote(packed.at[0], packed.at[1], qx_s, qx_r, partner)
    parts = lown if exact else snd
    main = [remote(parts.at[i], rcv.at[i], main_s.at[i], main_r.at[i], partner) for i in range(nchunk)]

    get_b.wait()
    get_g.wait()
    projected = jnp.dot(h32[...].astype(BF16), base_v[...], preferred_element_type=F32)

    sent_q.wait_recv()
    step_size = []
    lines = packed[1].astype(F32)
    for r in range(rows):
        line = jnp.where(wide_q, lines if r == 0 else pltpu.roll(lines, half, 1), 0.0)
        qoth[r] = line.astype(BF16)
        n = jnp.sum(jnp.abs(line), axis=1, keepdims=True)
        widest = jnp.maximum(widest, jnp.max(n, axis=0, keepdims=True))
        step_size.append(n * (CACHE_MOST * factor / LEVELS))

    def flag_copies(stage):
        src = fl.at[stage]
        if stage == 0:
            return [(src, fy.at[k - 1], fy_s.at[k - 1], fy_r.at[k - 1], y_peer(k)) for k in range(1, ys)]
        if stage == 1:
            return [(src, fx.at[k - 1], fx_s.at[k - 1], fx_r.at[k - 1], x_peer(k)) for k in range(1, xcs)]
        if stage == 2:
            return [(src, fz.at[k - 1], fz_s.at[k - 1], fz_r.at[k - 1], z_peer(k)) for k in range(1, zs)]
        return [(src, fp, fp_s, fp_r, partner)]

    def described(stage):
        return [
            pltpu.make_async_remote_copy(
                src_ref=src, dst_ref=dst, send_sem=send, recv_sem=recv, device_id=device, device_id_type=MESH
            )
            for src, dst, send, recv, device in flag_copies(stage)
        ]

    def flag_step(stage):
        if exact:
            return

        @pl.when(first)
        def _():
            if stage == 0:
                fl[0] = jnp.broadcast_to(widest, (8, HD))
            else:
                largest = fl[stage - 1]
                for copy, arrived in zip(described(stage - 1), flag_copies(stage - 1)):
                    copy.wait_recv()
                    largest = jnp.maximum(largest, arrived[1][...])
                fl[stage] = largest
            for copy in described(stage):
                copy.start()

    flag_step(0)

    for copy in sent_h:
        copy.wait_recv()
    for copy in sent_w:
        copy.wait_recv()
    mine = hs[zl].astype(F32)
    theirs = [hr[k].astype(F32) for k in range(zs - 1)]
    gathered = w_v[...]
    weights = gathered.reshape(own_blocks * BLOCK, HD)
    total = None
    for b in range(own_blocks):
        stacked = jnp.concatenate([part[b * 8 : (b + 1) * 8] for part in [mine] + theirs], axis=0).astype(BF16)
        term = jnp.dot(stacked, weights[b * BLOCK : (b + 1) * BLOCK], preferred_element_type=F32)
        term = term * scales[0, zl * own_blocks + b]
        total = term if total is None else total + term
    projected = projected + total[0:8]
    for k in range(1, zs):
        ysend[k] = total[k * 8 : (k + 1) * 8]
    ysend[0] = projected
    sent_p = [remote(ysend.at[0], yrecv.at[1, 0], p2_s.at[1, 0], p2_r.at[1, 0], partner)]
    for k in range(1, zs):
        for side, device in enumerate((z_peer(zs - k), other_z_peer(zs - k))):
            sent_p.append(remote(ysend.at[k], yrecv.at[side, k], p2_s.at[side, k], p2_r.at[side, k], device))

    flag_step(1)

    top = [jnp.full((nq, 1), NEGATIVE, F32) for _ in range(rows)]
    den = [jnp.zeros((nq, 1), F32) for _ in range(rows)]
    acc = [jnp.zeros((nq, HD), F32) for _ in range(rows)]

    def merge(r, values, block):
        highest = jnp.maximum(top[r], jnp.max(values, axis=1, keepdims=True))
        weight = jnp.exp(values - highest)
        keep = jnp.exp(top[r] - highest)
        den[r] = den[r] * keep + jnp.sum(weight, axis=1, keepdims=True)
        acc[r] = acc[r] * keep + jnp.dot(weight.astype(BF16), block, preferred_element_type=F32)
        top[r] = highest

    def take(i):
        r, c = i // per_row, i % per_row
        main[i].wait_recv()
        received = rcv[i] if exact else rcv[i].astype(jnp.int32).astype(F32) * step_size[r]
        values = lown[i] + received
        place = c * CHUNK + lax.broadcasted_iota(jnp.int32, (nq, CHUNK), 1)
        values = jnp.where(place < lens[r], values, NEGATIVE)
        merge(r, values, cache_v[r, c * CHUNK : (c + 1) * CHUNK, :])

    late = LATE
    for i in range(late):
        if i in FLAG_STEPS:
            flag_step(FLAG_STEPS[i])
        take(i)

    for copy in sent_p:
        copy.wait_recv()
    other = yrecv[1, 0]
    for k in range(1, zs):
        projected = projected + yrecv[0, k]
        other = other + yrecv[1, k]
    is_key = lane < half
    squares = jnp.sum(jnp.where(is_key, projected * projected, 0.0), axis=1, keepdims=True)
    squares = squares + jnp.sum(jnp.where(is_key, other * other, 0.0), axis=1, keepdims=True)
    inverse = lax.rsqrt(squares / HD + EPSILON)
    gains = jnp.broadcast_to(gain_v[...], (8, HD))
    swapped = pltpu.roll(gains, half, 1)
    own_gain = jnp.where(first, gains, swapped)
    other_gain = jnp.where(first, swapped, gains)
    entries = jnp.where(is_key, projected * inverse * own_gain, projected)
    other_keys = jnp.where(is_key, other * inverse * other_gain, 0.0)
    for s in range(steps):
        both_out[s, :, 0:HD] = entries[s * rows : (s + 1) * rows, :].astype(BF16)
    blank = jnp.zeros((8, HD), F32)
    own16 = jnp.concatenate([entries, blank], axis=0).astype(BF16)
    other16 = jnp.concatenate([other_keys, blank], axis=0).astype(BF16)
    column = lax.broadcasted_iota(jnp.int32, (nq, 16), 1)
    step_of = lax.broadcasted_iota(jnp.int32, (nq, 16), 0) // group
    for r in range(rows):
        fresh = lax.dot_general(qbf[r], own16, (((1,), (1,)), ((), ())), preferred_element_type=F32)
        fresh = fresh + lax.dot_general(qoth[r], other16, (((1,), (1,)), ((), ())), preferred_element_type=F32)
        allowed = (column % rows == r) & (column // rows <= step_of)
        merge(r, jnp.where(allowed, fresh * factor, NEGATIVE), own16)

    for i in range(late, nchunk):
        take(i)

    result = [acc[r] / den[r] for r in range(rows)]
    right = (lane >= half) == odd
    for s in range(steps):
        lines = []
        for r in range(rows):
            part = result[r][s * group : (s + 1) * group, :]
            part = jnp.where(odd, part, pltpu.roll(part, half, 1))
            part = jnp.where(right, part, 0.0)
            lines.append(
                [
                    jnp.sum(jnp.where(sub // 2 == j, part, 0.0), axis=0, keepdims=True)
                    for j in range(group * half // HD)
                ]
            )
        for j in range(group * half // HD):
            both_out[s, :, (j + 1) * HD : (j + 2) * HD] = jnp.concatenate([line[j] for line in lines], axis=0).astype(BF16)

    if not exact:

        @pl.when(first)
        def _():
            flag_out[...] = fl[3]
            for stage in range(4):
                for copy in described(stage):
                    copy.wait_send()

        @pl.when(jnp.logical_not(first))
        def _():
            described(3)[0].wait_recv()
            flag_out[...] = fp[...]

    for copy in main + [sent_q] + sent_h + sent_w + sent_p:
        copy.wait_send()


def fused(sizes, exact, hidden, base_kv, delta_codes, block_scales, key_gain, queries, kv_cache, lengths):
    zs, xcs, ys = sizes
    step_count, row_count, width = hidden.shape
    cache_length = kv_cache.shape[1]
    nq = step_count * 8
    nchunk = row_count * cache_length // CHUNK
    own_blocks = width // BLOCK // zs
    dma = pltpu.SemaphoreType.DMA
    any_space = pl.BlockSpec(memory_space=pl.ANY)
    smem = pl.BlockSpec(memory_space=pltpu.SMEM)
    vmem = pl.BlockSpec(memory_space=pltpu.VMEM)
    return pl.pallas_call(
        functools.partial(pair_kernel, zs, xcs, ys, exact),
        out_shape=(
            jax.ShapeDtypeStruct((step_count, row_count, HD + queries.shape[2]), BF16),
        )
        + (() if exact else (jax.ShapeDtypeStruct((8, HD), F32),)),
        in_specs=[any_space, any_space, any_space, smem, any_space, any_space, any_space, smem],
        out_specs=(vmem,) if exact else (vmem, vmem),
        scratch_shapes=[
            pltpu.VMEM(queries.shape, BF16),
            pltpu.VMEM(hidden.shape, BF16),
            pltpu.VMEM(base_kv.shape, BF16),
            pltpu.VMEM((1, HD), F32),
            pltpu.VMEM(kv_cache.shape, BF16),
            pltpu.VMEM((xcs,) + delta_codes.shape, BF16),
            pltpu.VMEM((row_count, nq, HD), F32),
            pltpu.VMEM((row_count, nq, HD), BF16),
            pltpu.VMEM((2, nq, HD), BF16),
            pltpu.VMEM((row_count, nq, HD), BF16),
            pltpu.VMEM((step_count * row_count, width), F32),
            pltpu.VMEM((zs, own_blocks * 8, BLOCK), BF16),
            pltpu.VMEM((zs - 1, own_blocks * 8, BLOCK), BF16),
            pltpu.VMEM((nchunk, nq, CHUNK), F32),
            pltpu.VMEM((1, nq, HD) if exact else (nchunk, nq, CHUNK), jnp.int16),
            pltpu.VMEM((nchunk, nq, CHUNK), F32 if exact else jnp.int16),
            pltpu.VMEM((zs, 8, HD), F32),
            pltpu.VMEM((2, zs, 8, HD), F32),
            pltpu.VMEM((4, 8, HD), F32),
            pltpu.VMEM((ys - 1, 8, HD), F32),
            pltpu.VMEM((xcs - 1, 8, HD), F32),
            pltpu.VMEM((zs - 1, 8, HD), F32),
            pltpu.VMEM((8, HD), F32),
            dma((5,)),
            dma((nchunk,)),
            dma((nchunk,)),
            dma((nchunk,)),
            dma,
            dma,
            dma((xcs - 1,)),
            dma((xcs - 1,)),
            dma((zs - 1,)),
            dma((zs - 1,)),
            dma((2, zs)),
            dma((2, zs)),
            dma((ys - 1,)),
            dma((ys - 1,)),
            dma((xcs - 1,)),
            dma((xcs - 1,)),
            dma((zs - 1,)),
            dma((zs - 1,)),
            dma,
            dma,
        ],
        compiler_params=pltpu.CompilerParams(
            collective_id=1 if exact else 0, has_side_effects=True
        ),
    )(hidden, base_kv, delta_codes, block_scales.T, key_gain.reshape(1, HD), queries, kv_cache, lengths)


def local(sizes, *args):
    both, widest = fused(sizes, False, *args)
    both = lax.cond(
        widest[0, 0] <= NORM_LIMIT,
        lambda args, fast: fast,
        lambda args, fast: fused(sizes, True, *args)[0],
        args,
        both,
    )
    return both[:, :, :HD], both[:, :, HD:]


def solution(mesh):
    fsdp, tp = mesh.shape["fsdp"], mesh.shape["tp"]
    sizes = (4, fsdp // 4, tp // 2)
    in_specs = (
        P(None, "fsdp", None),
        P(None, "tp"),
        P("fsdp", "tp"),
        P(None, "tp"),
        P(),
        P(None, "fsdp", "tp"),
        P("fsdp", None, "tp"),
        P("fsdp"),
    )
    out_specs = (P(None, "fsdp", "tp"), P(None, "fsdp", "tp"))
    return jax.shard_map(
        functools.partial(local, sizes), mesh=mesh, in_specs=in_specs, out_specs=out_specs, check_vma=False
    )
```

```python
import functools
import math

import jax
import jax.numpy as jnp
from jax import lax
from jax.experimental import pallas as pl
from jax.experimental.pallas import tpu as pltpu
from jax.sharding import PartitionSpec as P

HD = 128
BLOCK = 128


EPSILON = 1e-06
NEGATIVE = -1e30

CACHE_MOST = 6.0
NORM_LIMIT = 480.0
LEVELS = 32760.0

MESH = pl.DeviceIdType.MESH
F32 = jnp.float32
BF16 = jnp.bfloat16
CHUNK = 1024
LATE = 6
EARLY = 5
FLAG_STEPS = {2: 2, 5: 3}


def pair_kernel(
    zs, xcs, ys, exact,
    hid, base, codes, scales, gain, qry, cache, lens,
    *refs,
):
    both_out, refs = refs[0], refs[1:]
    if not exact:
        flag_out, refs = refs[0], refs[1:]
    (
    qv, hv, base_v, gain_v, cache_v, w_v, q32, qbf, packed, qoth, h32, hs, hr, lown, snd, rcv, ysend, yrecv,
    fl, fy, fx, fz, fp,
    loc_sem, cache_sem, main_s, main_r, qx_s, qx_r, ag_s, ag_r, p1_s, p1_r, p2_s, p2_r,
    fy_s, fy_r, fx_s, fx_r, fz_s, fz_r, fp_s, fp_r,
    ) = refs
    f = lax.axis_index("fsdp")
    t = lax.axis_index("tp")
    zl = f // xcs
    xc = lax.rem(f, xcs)
    zh = t // ys
    y = lax.rem(t, ys)
    rows = cache.shape[0]
    steps = qry.shape[0]
    group = 8
    half = HD // 2
    nq = steps * group
    per_row = cache.shape[1] // CHUNK
    nchunk = rows * per_row
    factor = 1.0 / math.sqrt(HD)

    partner = (f, (1 - zh) * ys + y)

    def z_peer(k):
        return (lax.rem(zl + k, zs) * xcs + xc, t)

    def other_z_peer(k):
        return (lax.rem(zl + k, zs) * xcs + xc, (1 - zh) * ys + y)

    def x_peer(k):
        return (zl * xcs + lax.rem(xc + k, xcs), t)

    def y_peer(k):
        return (f, zh * ys + lax.rem(y + k, ys))

    barrier = pltpu.get_barrier_semaphore()
    everyone = (
        [z_peer(k) for k in range(1, zs)]
        + [x_peer(k) for k in range(1, xcs)]
        + [partner]
        + [other_z_peer(k) for k in range(1, zs)]
    )
    for device in everyone:
        pl.semaphore_signal(barrier, inc=1, device_id=device, device_id_type=MESH)

    first = zh == 0
    if not exact:

        @pl.when(first)
        def _():
            for k in range(1, ys):
                pl.semaphore_signal(barrier, inc=1, device_id=y_peer(k), device_id_type=MESH)

    get_q = pltpu.make_async_copy(qry, qv, loc_sem.at[0])
    get_h = pltpu.make_async_copy(hid, hv, loc_sem.at[1])
    get_w = pltpu.make_async_copy(codes, w_v.at[xc], loc_sem.at[2])
    get_b = pltpu.make_async_copy(base, base_v, loc_sem.at[3])
    get_g = pltpu.make_async_copy(gain, gain_v, loc_sem.at[4])
    get_q.start()
    get_c = []
    for i in range(nchunk):
        r, c = i // per_row, i % per_row
        part = pl.ds(c * CHUNK, CHUNK)
        get_c.append(pltpu.make_async_copy(cache.at[r, part], cache_v.at[r, part], cache_sem.at[i]))
    get_c[0].start()
    get_h.start()
    for copy in get_c[1:]:
        copy.start()
    get_w.start()
    get_b.start()
    get_g.start()

    get_q.wait()
    lane512 = lax.broadcasted_iota(jnp.int32, (8, group * half), 1)
    sub512 = lax.broadcasted_iota(jnp.int32, (8, group * half), 0)
    own512 = (lane512 // half) == sub512
    sub = lax.broadcasted_iota(jnp.int32, (8, HD), 0)
    lane = lax.broadcasted_iota(jnp.int32, (8, HD), 1)
    odd = (sub % 2) == 1
    for s in range(steps):
        both = qv[s].astype(F32)
        for r in range(rows):
            spread = jnp.broadcast_to(both[r : r + 1], (8, group * half))
            spread = jnp.where(own512, spread, 0.0)
            folded = spread[:, 0:HD]
            for j in range(1, group * half // HD):
                folded = folded + spread[:, j * HD : (j + 1) * HD]
            folded = jnp.where(odd, pltpu.roll(folded, half, 1), folded)
            q32[r, s * group : (s + 1) * group, :] = folded
    norms = []
    for r in range(rows):
        qbf[r] = q32[r].astype(BF16)
        norms.append(jnp.sum(jnp.abs(q32[r]), axis=1, keepdims=True))
    widest = jnp.max(norms[0], axis=0, keepdims=True)
    for r in range(1, rows):
        widest = jnp.maximum(widest, jnp.max(norms[r], axis=0, keepdims=True))
    wide_q = lax.broadcasted_iota(jnp.int32, (nq, HD), 1) < half
    packed[0] = (q32[0] + pltpu.roll(q32[1], half, 1)).astype(BF16)
    to_code = [LEVELS / (CACHE_MOST * jnp.maximum(n, 1e-30)) for n in norms]

    def logits(i):
        r, c = i // per_row, i % per_row
        get_c[i].wait()
        block = cache_v[r, c * CHUNK : (c + 1) * CHUNK, :]
        raw = lax.dot_general(qbf[r], block, (((1,), (1,)), ((), ())), preferred_element_type=F32)
        lown[i] = raw * factor
        if not exact:
            snd[i] = jnp.round(raw * to_code[r]).astype(jnp.int32).astype(jnp.int16)

    for i in range(nchunk):
        logits(i)

    get_h.wait()
    for s in range(steps):
        h32[s * rows : (s + 1) * rows, :] = hv[s].astype(F32)
    blocks = h32.shape[1] // BLOCK
    own_blocks = blocks // zs
    for j in range(blocks // 2):
        low = h32[:, 2 * j * BLOCK : (2 * j + 1) * BLOCK]
        high = h32[:, (2 * j + 1) * BLOCK : (2 * j + 2) * BLOCK]
        hs[(2 * j) // own_blocks, (2 * j % own_blocks) * 8 : (2 * j % own_blocks) * 8 + 16, :] = jnp.concatenate(
            [low, high], axis=0
        ).astype(BF16)

    get_w.wait()
    pl.semaphore_wait(barrier, len(everyone) + (0 if exact else (1 - zh) * (ys - 1)))

    def remote(src, dst, send, recv, device):
        copy = pltpu.make_async_remote_copy(
            src_ref=src, dst_ref=dst, send_sem=send, recv_sem=recv, device_id=device, device_id_type=MESH
        )
        copy.start()
        return copy

    sent_h = [
        remote(hs.at[lax.rem(zl + k, zs)], hr.at[k - 1], p1_s.at[k - 1], p1_r.at[k - 1], z_peer(k))
        for k in range(1, zs)
    ]
    sent_w = [
        remote(w_v.at[xc], w_v.at[xc], ag_s.at[k - 1], ag_r.at[k - 1], x_peer(k)) for k in range(1, xcs)
    ]
    sent_q = remote(packed.at[0], packed.at[1], qx_s, qx_r, partner)
    parts = lown if exact else snd

    def send_main(low, high):
        return [
            remote(parts.at[i], rcv.at[i], main_s.at[i], main_r.at[i], partner) for i in range(low, high)
        ]

    main = send_main(0, EARLY)

    get_b.wait()
    get_g.wait()
    projected = jnp.dot(h32[...].astype(BF16), base_v[...], preferred_element_type=F32)

    sent_q.wait_recv()
    step_size = []
    lines = packed[1].astype(F32)
    for r in range(rows):
        line = jnp.where(wide_q, lines if r == 0 else pltpu.roll(lines, half, 1), 0.0)
        qoth[r] = line.astype(BF16)
        n = jnp.sum(jnp.abs(line), axis=1, keepdims=True)
        widest = jnp.maximum(widest, jnp.max(n, axis=0, keepdims=True))
        step_size.append(n * (CACHE_MOST * factor / LEVELS))

    def flag_copies(stage):
        src = fl.at[stage]
        if stage == 0:
            return [(src, fy.at[k - 1], fy_s.at[k - 1], fy_r.at[k - 1], y_peer(k)) for k in range(1, ys)]
        if stage == 1:
            return [(src, fx.at[k - 1], fx_s.at[k - 1], fx_r.at[k - 1], x_peer(k)) for k in range(1, xcs)]
        if stage == 2:
            return [(src, fz.at[k - 1], fz_s.at[k - 1], fz_r.at[k - 1], z_peer(k)) for k in range(1, zs)]
        return [(src, fp, fp_s, fp_r, partner)]

    def described(stage):
        return [
            pltpu.make_async_remote_copy(
                src_ref=src, dst_ref=dst, send_sem=send, recv_sem=recv, device_id=device, device_id_type=MESH
            )
            for src, dst, send, recv, device in flag_copies(stage)
        ]

    def flag_step(stage):
        if exact:
            return

        @pl.when(first)
        def _():
            if stage == 0:
                fl[0] = jnp.broadcast_to(widest, (8, HD))
            else:
                largest = fl[stage - 1]
                for copy, arrived in zip(described(stage - 1), flag_copies(stage - 1)):
                    copy.wait_recv()
                    largest = jnp.maximum(largest, arrived[1][...])
                fl[stage] = largest
            for copy in described(stage):
                copy.start()

    flag_step(0)

    for copy in sent_h:
        copy.wait_recv()
    for copy in sent_w:
        copy.wait_recv()
    mine = hs[zl].astype(F32)
    theirs = [hr[k].astype(F32) for k in range(zs - 1)]
    gathered = w_v[...]
    weights = gathered.reshape(own_blocks * BLOCK, HD)
    total = None
    for b in range(own_blocks):
        stacked = jnp.concatenate([part[b * 8 : (b + 1) * 8] for part in [mine] + theirs], axis=0).astype(BF16)
        term = jnp.dot(stacked, weights[b * BLOCK : (b + 1) * BLOCK], preferred_element_type=F32)
        term = term * scales[0, zl * own_blocks + b]
        total = term if total is None else total + term
    projected = projected + total[0:8]
    for k in range(1, zs):
        ysend[k] = total[k * 8 : (k + 1) * 8]
    ysend[0] = projected
    sent_p = [remote(ysend.at[0], yrecv.at[1, 0], p2_s.at[1, 0], p2_r.at[1, 0], partner)]
    for k in range(1, zs):
        for side, device in enumerate((z_peer(zs - k), other_z_peer(zs - k))):
            sent_p.append(remote(ysend.at[k], yrecv.at[side, k], p2_s.at[side, k], p2_r.at[side, k], device))

    main += send_main(EARLY, nchunk)
    flag_step(1)

    top = [jnp.full((nq, 1), NEGATIVE, F32) for _ in range(rows)]
    den = [jnp.zeros((nq, 1), F32) for _ in range(rows)]
    acc = [jnp.zeros((nq, HD), F32) for _ in range(rows)]

    def merge(r, values, block):
        highest = jnp.maximum(top[r], jnp.max(values, axis=1, keepdims=True))
        weight = jnp.exp(values - highest)
        keep = jnp.exp(top[r] - highest)
        den[r] = den[r] * keep + jnp.sum(weight, axis=1, keepdims=True)
        acc[r] = acc[r] * keep + jnp.dot(weight.astype(BF16), block, preferred_element_type=F32)
        top[r] = highest

    def take(i):
        r, c = i // per_row, i % per_row
        main[i].wait_recv()
        received = rcv[i] if exact else rcv[i].astype(jnp.int32).astype(F32) * step_size[r]
        values = lown[i] + received
        place = c * CHUNK + lax.broadcasted_iota(jnp.int32, (nq, CHUNK), 1)
        values = jnp.where(place < lens[r], values, NEGATIVE)
        merge(r, values, cache_v[r, c * CHUNK : (c + 1) * CHUNK, :])

    late = LATE
    for i in range(late):
        if i in FLAG_STEPS:
            flag_step(FLAG_STEPS[i])
        take(i)

    for copy in sent_p:
        copy.wait_recv()
    other = yrecv[1, 0]
    for k in range(1, zs):
        projected = projected + yrecv[0, k]
        other = other + yrecv[1, k]
    is_key = lane < half
    squares = jnp.sum(jnp.where(is_key, projected * projected, 0.0), axis=1, keepdims=True)
    squares = squares + jnp.sum(jnp.where(is_key, other * other, 0.0), axis=1, keepdims=True)
    inverse = lax.rsqrt(squares / HD + EPSILON)
    gains = jnp.broadcast_to(gain_v[...], (8, HD))
    swapped = pltpu.roll(gains, half, 1)
    own_gain = jnp.where(first, gains, swapped)
    other_gain = jnp.where(first, swapped, gains)
    entries = jnp.where(is_key, projected * inverse * own_gain, projected)
    other_keys = jnp.where(is_key, other * inverse * other_gain, 0.0)
    for s in range(steps):
        both_out[s, :, 0:HD] = entries[s * rows : (s + 1) * rows, :].astype(BF16)
    blank = jnp.zeros((8, HD), F32)
    own16 = jnp.concatenate([entries, blank], axis=0).astype(BF16)
    other16 = jnp.concatenate([other_keys, blank], axis=0).astype(BF16)
    column = lax.broadcasted_iota(jnp.int32, (nq, 16), 1)
    step_of = lax.broadcasted_iota(jnp.int32, (nq, 16), 0) // group
    for r in range(rows):
        fresh = lax.dot_general(qbf[r], own16, (((1,), (1,)), ((), ())), preferred_element_type=F32)
        fresh = fresh + lax.dot_general(qoth[r], other16, (((1,), (1,)), ((), ())), preferred_element_type=F32)
        allowed = (column % rows == r) & (column // rows <= step_of)
        merge(r, jnp.where(allowed, fresh * factor, NEGATIVE), own16)

    for i in range(late, nchunk):
        take(i)

    result = [acc[r] / den[r] for r in range(rows)]
    right = (lane >= half) == odd
    for s in range(steps):
        lines = []
        for r in range(rows):
            part = result[r][s * group : (s + 1) * group, :]
            part = jnp.where(odd, part, pltpu.roll(part, half, 1))
            part = jnp.where(right, part, 0.0)
            lines.append(
                [
                    jnp.sum(jnp.where(sub // 2 == j, part, 0.0), axis=0, keepdims=True)
                    for j in range(group * half // HD)
                ]
            )
        for j in range(group * half // HD):
            both_out[s, :, (j + 1) * HD : (j + 2) * HD] = jnp.concatenate([line[j] for line in lines], axis=0).astype(BF16)

    if not exact:

        @pl.when(first)
        def _():
            fp[...] = fl[3]
            for stage in range(4):
                for copy in described(stage):
                    copy.wait_send()

        @pl.when(jnp.logical_not(first))
        def _():
            described(3)[0].wait_recv()

        flag_out[0] = jnp.where(jnp.max(fp[...]) <= NORM_LIMIT, 1, 0).astype(jnp.int32)

    for copy in main + [sent_q] + sent_h + sent_w + sent_p:
        copy.wait_send()


def fused(sizes, exact, hidden, base_kv, delta_codes, block_scales, key_gain, queries, kv_cache, lengths):
    zs, xcs, ys = sizes
    step_count, row_count, width = hidden.shape
    cache_length = kv_cache.shape[1]
    nq = step_count * 8
    nchunk = row_count * cache_length // CHUNK
    own_blocks = width // BLOCK // zs
    dma = pltpu.SemaphoreType.DMA
    any_space = pl.BlockSpec(memory_space=pl.ANY)
    smem = pl.BlockSpec(memory_space=pltpu.SMEM)
    vmem = pl.BlockSpec(memory_space=pltpu.VMEM)
    return pl.pallas_call(
        functools.partial(pair_kernel, zs, xcs, ys, exact),
        out_shape=(
            jax.ShapeDtypeStruct((step_count, row_count, HD + queries.shape[2]), BF16),
        )
        + (() if exact else (jax.ShapeDtypeStruct((1,), jnp.int32),)),
        in_specs=[any_space, any_space, any_space, smem, any_space, any_space, any_space, smem],
        out_specs=(vmem,) if exact else (vmem, smem),
        scratch_shapes=[
            pltpu.VMEM(queries.shape, BF16),
            pltpu.VMEM(hidden.shape, BF16),
            pltpu.VMEM(base_kv.shape, BF16),
            pltpu.VMEM((1, HD), F32),
            pltpu.VMEM(kv_cache.shape, BF16),
            pltpu.VMEM((xcs,) + delta_codes.shape, BF16),
            pltpu.VMEM((row_count, nq, HD), F32),
            pltpu.VMEM((row_count, nq, HD), BF16),
            pltpu.VMEM((2, nq, HD), BF16),
            pltpu.VMEM((row_count, nq, HD), BF16),
            pltpu.VMEM((step_count * row_count, width), F32),
            pltpu.VMEM((zs, own_blocks * 8, BLOCK), BF16),
            pltpu.VMEM((zs - 1, own_blocks * 8, BLOCK), BF16),
            pltpu.VMEM((nchunk, nq, CHUNK), F32),
            pltpu.VMEM((1, nq, HD) if exact else (nchunk, nq, CHUNK), jnp.int16),
            pltpu.VMEM((nchunk, nq, CHUNK), F32 if exact else jnp.int16),
            pltpu.VMEM((zs, 8, HD), F32),
            pltpu.VMEM((2, zs, 8, HD), F32),
            pltpu.VMEM((4, 8, HD), F32),
            pltpu.VMEM((ys - 1, 8, HD), F32),
            pltpu.VMEM((xcs - 1, 8, HD), F32),
            pltpu.VMEM((zs - 1, 8, HD), F32),
            pltpu.VMEM((8, HD), F32),
            dma((5,)),
            dma((nchunk,)),
            dma((nchunk,)),
            dma((nchunk,)),
            dma,
            dma,
            dma((xcs - 1,)),
            dma((xcs - 1,)),
            dma((zs - 1,)),
            dma((zs - 1,)),
            dma((2, zs)),
            dma((2, zs)),
            dma((ys - 1,)),
            dma((ys - 1,)),
            dma((xcs - 1,)),
            dma((xcs - 1,)),
            dma((zs - 1,)),
            dma((zs - 1,)),
            dma,
            dma,
        ],
        compiler_params=pltpu.CompilerParams(
            collective_id=1 if exact else 0, has_side_effects=True
        ),
    )(hidden, base_kv, delta_codes, block_scales.T, key_gain.reshape(1, HD), queries, kv_cache, lengths)


def split_kernel(both, new_entries, attended):
    new_entries[...] = both[:, :, :HD]
    attended[...] = both[:, :, HD:]


def local(sizes, *args):
    both, narrow = fused(sizes, False, *args)
    both = lax.cond(
        narrow[0] != 0,
        lambda args, fast: fast,
        lambda args, fast: fused(sizes, True, *args)[0],
        args,
        both,
    )
    return pl.pallas_call(
        split_kernel,
        out_shape=(
            jax.ShapeDtypeStruct(both.shape[:2] + (HD,), BF16),
            jax.ShapeDtypeStruct(both.shape[:2] + (both.shape[2] - HD,), BF16),
        ),
    )(both)


def solution(mesh):
    fsdp, tp = mesh.shape["fsdp"], mesh.shape["tp"]
    sizes = (4, fsdp // 4, tp // 2)
    in_specs = (
        P(None, "fsdp", None),
        P(None, "tp"),
        P("fsdp", "tp"),
        P(None, "tp"),
        P(),
        P(None, "fsdp", "tp"),
        P("fsdp", None, "tp"),
        P("fsdp"),
    )
    out_specs = (P(None, "fsdp", "tp"), P(None, "fsdp", "tp"))
    return jax.shard_map(
        functools.partial(local, sizes), mesh=mesh, in_specs=in_specs, out_specs=out_specs, check_vma=False
    )
```

```python
import functools
import math

import jax
import jax.numpy as jnp
from jax import lax
from jax.experimental import pallas as pl
from jax.experimental.pallas import tpu as pltpu
from jax.sharding import PartitionSpec as P

HD = 128
BLOCK = 128


EPSILON = 1e-06
NEGATIVE = -1e30

CACHE_MOST = 6.0
NORM_LIMIT = 480.0
LEVELS = 32760.0

MESH = pl.DeviceIdType.MESH
F32 = jnp.float32
BF16 = jnp.bfloat16
CHUNK = 1024
LATE = 8
EARLY = 5
FLAG_STEPS = {2: 2, 7: 3}


def pair_kernel(
    zs, xcs, ys, exact,
    hid, base, codes, scales, gain, qry, cache, lens,
    *refs,
):
    both_out, refs = refs[0], refs[1:]
    if not exact:
        flag_out, refs = refs[0], refs[1:]
    (
    qv, hv, base_v, gain_v, cache_v, w_v, q32, qbf, packed, qoth, h32, hs, hr, lown, snd, rcv, ysend, yrecv,
    fl, fy, fx, fz, fp,
    loc_sem, cache_sem, main_s, main_r, qx_s, qx_r, ag_s, ag_r, p1_s, p1_r, p2_s, p2_r,
    fy_s, fy_r, fx_s, fx_r, fz_s, fz_r, fp_s, fp_r,
    ) = refs
    f = lax.axis_index("fsdp")
    t = lax.axis_index("tp")
    zl = f // xcs
    xc = lax.rem(f, xcs)
    zh = t // ys
    y = lax.rem(t, ys)
    rows = cache.shape[0]
    steps = qry.shape[0]
    group = 8
    half = HD // 2
    nq = steps * group
    per_row = cache.shape[1] // CHUNK
    nchunk = rows * per_row
    factor = 1.0 / math.sqrt(HD)

    partner = (f, (1 - zh) * ys + y)

    def z_peer(k):
        return (lax.rem(zl + k, zs) * xcs + xc, t)

    def other_z_peer(k):
        return (lax.rem(zl + k, zs) * xcs + xc, (1 - zh) * ys + y)

    def x_peer(k):
        return (zl * xcs + lax.rem(xc + k, xcs), t)

    def y_peer(k):
        return (f, zh * ys + lax.rem(y + k, ys))

    barrier = pltpu.get_barrier_semaphore()
    everyone = (
        [z_peer(k) for k in range(1, zs)]
        + [x_peer(k) for k in range(1, xcs)]
        + [partner]
        + [other_z_peer(k) for k in range(1, zs)]
    )
    for device in everyone:
        pl.semaphore_signal(barrier, inc=1, device_id=device, device_id_type=MESH)

    first = zh == 0
    if not exact:

        @pl.when(first)
        def _():
            for k in range(1, ys):
                pl.semaphore_signal(barrier, inc=1, device_id=y_peer(k), device_id_type=MESH)

    get_q = pltpu.make_async_copy(qry, qv, loc_sem.at[0])
    get_h = pltpu.make_async_copy(hid, hv, loc_sem.at[1])
    get_w = pltpu.make_async_copy(codes, w_v.at[xc], loc_sem.at[2])
    get_b = pltpu.make_async_copy(base, base_v, loc_sem.at[3])
    get_g = pltpu.make_async_copy(gain, gain_v, loc_sem.at[4])
    get_q.start()
    get_c = []
    for i in range(nchunk):
        r, c = i // per_row, i % per_row
        part = pl.ds(c * CHUNK, CHUNK)
        get_c.append(pltpu.make_async_copy(cache.at[r, part], cache_v.at[r, part], cache_sem.at[i]))
    get_c[0].start()
    get_h.start()
    for copy in get_c[1:]:
        copy.start()
    get_w.start()
    get_b.start()
    get_g.start()

    get_q.wait()
    lane512 = lax.broadcasted_iota(jnp.int32, (8, group * half), 1)
    sub512 = lax.broadcasted_iota(jnp.int32, (8, group * half), 0)
    own512 = (lane512 // half) == sub512
    sub = lax.broadcasted_iota(jnp.int32, (8, HD), 0)
    lane = lax.broadcasted_iota(jnp.int32, (8, HD), 1)
    odd = (sub % 2) == 1
    for s in range(steps):
        both = qv[s].astype(F32)
        for r in range(rows):
            spread = jnp.broadcast_to(both[r : r + 1], (8, group * half))
            spread = jnp.where(own512, spread, 0.0)
            folded = spread[:, 0:HD]
            for j in range(1, group * half // HD):
                folded = folded + spread[:, j * HD : (j + 1) * HD]
            folded = jnp.where(odd, pltpu.roll(folded, half, 1), folded)
            q32[r, s * group : (s + 1) * group, :] = folded
    norms = []
    for r in range(rows):
        qbf[r] = q32[r].astype(BF16)
        norms.append(jnp.sum(jnp.abs(q32[r]), axis=1, keepdims=True))
    widest = jnp.max(norms[0], axis=0, keepdims=True)
    for r in range(1, rows):
        widest = jnp.maximum(widest, jnp.max(norms[r], axis=0, keepdims=True))
    wide_q = lax.broadcasted_iota(jnp.int32, (nq, HD), 1) < half
    packed[0] = (q32[0] + pltpu.roll(q32[1], half, 1)).astype(BF16)
    to_code = [LEVELS / (CACHE_MOST * jnp.maximum(n, 1e-30)) for n in norms]

    def logits(i):
        r, c = i // per_row, i % per_row
        get_c[i].wait()
        block = cache_v[r, c * CHUNK : (c + 1) * CHUNK, :]
        raw = lax.dot_general(qbf[r], block, (((1,), (1,)), ((), ())), preferred_element_type=F32)
        lown[i] = raw * factor
        if not exact:
            snd[i] = jnp.round(raw * to_code[r]).astype(jnp.int32).astype(jnp.int16)

    for i in range(nchunk):
        logits(i)

    get_h.wait()
    for s in range(steps):
        h32[s * rows : (s + 1) * rows, :] = hv[s].astype(F32)
    blocks = h32.shape[1] // BLOCK
    own_blocks = blocks // zs
    for j in range(blocks // 2):
        low = h32[:, 2 * j * BLOCK : (2 * j + 1) * BLOCK]
        high = h32[:, (2 * j + 1) * BLOCK : (2 * j + 2) * BLOCK]
        hs[(2 * j) // own_blocks, (2 * j % own_blocks) * 8 : (2 * j % own_blocks) * 8 + 16, :] = jnp.concatenate(
            [low, high], axis=0
        ).astype(BF16)

    get_w.wait()
    pl.semaphore_wait(barrier, len(everyone) + (0 if exact else (1 - zh) * (ys - 1)))

    def remote(src, dst, send, recv, device):
        copy = pltpu.make_async_remote_copy(
            src_ref=src, dst_ref=dst, send_sem=send, recv_sem=recv, device_id=device, device_id_type=MESH
        )
        copy.start()
        return copy

    sent_h = [
        remote(hs.at[lax.rem(zl + k, zs)], hr.at[k - 1], p1_s.at[k - 1], p1_r.at[k - 1], z_peer(k))
        for k in range(1, zs)
    ]
    sent_w = [
        remote(w_v.at[xc], w_v.at[xc], ag_s.at[k - 1], ag_r.at[k - 1], x_peer(k)) for k in range(1, xcs)
    ]
    sent_q = remote(packed.at[0], packed.at[1], qx_s, qx_r, partner)
    parts = lown if exact else snd

    def send_main(low, high):
        return [
            remote(parts.at[i], rcv.at[i], main_s.at[i], main_r.at[i], partner) for i in range(low, high)
        ]

    main = send_main(0, EARLY)

    get_b.wait()
    get_g.wait()
    projected = jnp.dot(h32[...].astype(BF16), base_v[...], preferred_element_type=F32)

    sent_q.wait_recv()
    step_size = []
    lines = packed[1].astype(F32)
    for r in range(rows):
        line = jnp.where(wide_q, lines if r == 0 else pltpu.roll(lines, half, 1), 0.0)
        qoth[r] = line.astype(BF16)
        n = jnp.sum(jnp.abs(line), axis=1, keepdims=True)
        widest = jnp.maximum(widest, jnp.max(n, axis=0, keepdims=True))
        step_size.append(n * (CACHE_MOST * factor / LEVELS))

    def flag_copies(stage):
        src = fl.at[stage]
        if stage == 0:
            return [(src, fy.at[k - 1], fy_s.at[k - 1], fy_r.at[k - 1], y_peer(k)) for k in range(1, ys)]
        if stage == 1:
            return [(src, fx.at[k - 1], fx_s.at[k - 1], fx_r.at[k - 1], x_peer(k)) for k in range(1, xcs)]
        if stage == 2:
            return [(src, fz.at[k - 1], fz_s.at[k - 1], fz_r.at[k - 1], z_peer(k)) for k in range(1, zs)]
        return [(src, fp, fp_s, fp_r, partner)]

    def described(stage):
        return [
            pltpu.make_async_remote_copy(
                src_ref=src, dst_ref=dst, send_sem=send, recv_sem=recv, device_id=device, device_id_type=MESH
            )
            for src, dst, send, recv, device in flag_copies(stage)
        ]

    def flag_step(stage):
        if exact:
            return

        @pl.when(first)
        def _():
            if stage == 0:
                fl[0] = jnp.broadcast_to(widest, (8, HD))
            else:
                largest = fl[stage - 1]
                for copy, arrived in zip(described(stage - 1), flag_copies(stage - 1)):
                    copy.wait_recv()
                    largest = jnp.maximum(largest, arrived[1][...])
                fl[stage] = largest
            for copy in described(stage):
                copy.start()

    flag_step(0)

    for copy in sent_h:
        copy.wait_recv()
    for copy in sent_w:
        copy.wait_recv()
    mine = hs[zl].astype(F32)
    theirs = [hr[k].astype(F32) for k in range(zs - 1)]
    gathered = w_v[...]
    weights = gathered.reshape(own_blocks * BLOCK, HD)
    total = None
    for b in range(own_blocks):
        stacked = jnp.concatenate([part[b * 8 : (b + 1) * 8] for part in [mine] + theirs], axis=0).astype(BF16)
        term = jnp.dot(stacked, weights[b * BLOCK : (b + 1) * BLOCK], preferred_element_type=F32)
        term = term * scales[0, zl * own_blocks + b]
        total = term if total is None else total + term
    projected = projected + total[0:8]
    for k in range(1, zs):
        ysend[k] = total[k * 8 : (k + 1) * 8]
    ysend[0] = projected
    sent_p = [remote(ysend.at[0], yrecv.at[1, 0], p2_s.at[1, 0], p2_r.at[1, 0], partner)]
    for k in range(1, zs):
        for side, device in enumerate((z_peer(zs - k), other_z_peer(zs - k))):
            sent_p.append(remote(ysend.at[k], yrecv.at[side, k], p2_s.at[side, k], p2_r.at[side, k], device))

    main += send_main(EARLY, nchunk)
    flag_step(1)

    top = [jnp.full((nq, 1), NEGATIVE, F32) for _ in range(rows)]
    den = [jnp.zeros((nq, 1), F32) for _ in range(rows)]
    acc = [jnp.zeros((nq, HD), F32) for _ in range(rows)]

    def merge(r, values, block):
        highest = jnp.maximum(top[r], jnp.max(values, axis=1, keepdims=True))
        weight = jnp.exp(values - highest)
        keep = jnp.exp(top[r] - highest)
        den[r] = den[r] * keep + jnp.sum(weight, axis=1, keepdims=True)
        acc[r] = acc[r] * keep + jnp.dot(weight.astype(BF16), block, preferred_element_type=F32)
        top[r] = highest

    def take(i):
        r, c = i // per_row, i % per_row
        main[i].wait_recv()
        received = rcv[i] if exact else rcv[i].astype(jnp.int32).astype(F32) * step_size[r]
        values = lown[i] + received
        place = c * CHUNK + lax.broadcasted_iota(jnp.int32, (nq, CHUNK), 1)
        values = jnp.where(place < lens[r], values, NEGATIVE)
        merge(r, values, cache_v[r, c * CHUNK : (c + 1) * CHUNK, :])

    late = LATE
    for i in range(late):
        if i in FLAG_STEPS:
            flag_step(FLAG_STEPS[i])
        take(i)

    for copy in sent_p:
        copy.wait_recv()
    other = yrecv[1, 0]
    for k in range(1, zs):
        projected = projected + yrecv[0, k]
        other = other + yrecv[1, k]
    is_key = lane < half
    squares = jnp.sum(jnp.where(is_key, projected * projected, 0.0), axis=1, keepdims=True)
    squares = squares + jnp.sum(jnp.where(is_key, other * other, 0.0), axis=1, keepdims=True)
    inverse = lax.rsqrt(squares / HD + EPSILON)
    gains = jnp.broadcast_to(gain_v[...], (8, HD))
    swapped = pltpu.roll(gains, half, 1)
    own_gain = jnp.where(first, gains, swapped)
    other_gain = jnp.where(first, swapped, gains)
    entries = jnp.where(is_key, projected * inverse * own_gain, projected)
    other_keys = jnp.where(is_key, other * inverse * other_gain, 0.0)
    for s in range(steps):
        both_out[s, :, 0:HD] = entries[s * rows : (s + 1) * rows, :].astype(BF16)
    blank = jnp.zeros((8, HD), F32)
    own16 = jnp.concatenate([entries, blank], axis=0).astype(BF16)
    other16 = jnp.concatenate([other_keys, blank], axis=0).astype(BF16)
    column = lax.broadcasted_iota(jnp.int32, (nq, 16), 1)
    step_of = lax.broadcasted_iota(jnp.int32, (nq, 16), 0) // group
    for r in range(rows):
        fresh = lax.dot_general(qbf[r], own16, (((1,), (1,)), ((), ())), preferred_element_type=F32)
        fresh = fresh + lax.dot_general(qoth[r], other16, (((1,), (1,)), ((), ())), preferred_element_type=F32)
        allowed = (column % rows == r) & (column // rows <= step_of)
        merge(r, jnp.where(allowed, fresh * factor, NEGATIVE), own16)

    for i in range(late, nchunk):
        take(i)

    result = [acc[r] / den[r] for r in range(rows)]
    right = (lane >= half) == odd
    for s in range(steps):
        lines = []
        for r in range(rows):
            part = result[r][s * group : (s + 1) * group, :]
            part = jnp.where(odd, part, pltpu.roll(part, half, 1))
            part = jnp.where(right, part, 0.0)
            lines.append(
                [
                    jnp.sum(jnp.where(sub // 2 == j, part, 0.0), axis=0, keepdims=True)
                    for j in range(group * half // HD)
                ]
            )
        for j in range(group * half // HD):
            both_out[s, :, (j + 1) * HD : (j + 2) * HD] = jnp.concatenate([line[j] for line in lines], axis=0).astype(BF16)

    if not exact:

        @pl.when(first)
        def _():
            fp[...] = fl[3]
            for stage in range(4):
                for copy in described(stage):
                    copy.wait_send()

        @pl.when(jnp.logical_not(first))
        def _():
            described(3)[0].wait_recv()

        flag_out[0] = jnp.where(jnp.max(fp[...]) <= NORM_LIMIT, 1, 0).astype(jnp.int32)

    for copy in main + [sent_q] + sent_h + sent_w + sent_p:
        copy.wait_send()


def fused(sizes, exact, hidden, base_kv, delta_codes, block_scales, key_gain, queries, kv_cache, lengths):
    zs, xcs, ys = sizes
    step_count, row_count, width = hidden.shape
    cache_length = kv_cache.shape[1]
    nq = step_count * 8
    nchunk = row_count * cache_length // CHUNK
    own_blocks = width // BLOCK // zs
    dma = pltpu.SemaphoreType.DMA
    any_space = pl.BlockSpec(memory_space=pl.ANY)
    smem = pl.BlockSpec(memory_space=pltpu.SMEM)
    vmem = pl.BlockSpec(memory_space=pltpu.VMEM)
    return pl.pallas_call(
        functools.partial(pair_kernel, zs, xcs, ys, exact),
        out_shape=(
            jax.ShapeDtypeStruct((step_count, row_count, HD + queries.shape[2]), BF16),
        )
        + (() if exact else (jax.ShapeDtypeStruct((1,), jnp.int32),)),
        in_specs=[any_space, any_space, any_space, smem, any_space, any_space, any_space, smem],
        out_specs=(vmem,) if exact else (vmem, smem),
        scratch_shapes=[
            pltpu.VMEM(queries.shape, BF16),
            pltpu.VMEM(hidden.shape, BF16),
            pltpu.VMEM(base_kv.shape, BF16),
            pltpu.VMEM((1, HD), F32),
            pltpu.VMEM(kv_cache.shape, BF16),
            pltpu.VMEM((xcs,) + delta_codes.shape, BF16),
            pltpu.VMEM((row_count, nq, HD), F32),
            pltpu.VMEM((row_count, nq, HD), BF16),
            pltpu.VMEM((2, nq, HD), BF16),
            pltpu.VMEM((row_count, nq, HD), BF16),
            pltpu.VMEM((step_count * row_count, width), F32),
            pltpu.VMEM((zs, own_blocks * 8, BLOCK), BF16),
            pltpu.VMEM((zs - 1, own_blocks * 8, BLOCK), BF16),
            pltpu.VMEM((nchunk, nq, CHUNK), F32),
            pltpu.VMEM((1, nq, HD) if exact else (nchunk, nq, CHUNK), jnp.int16),
            pltpu.VMEM((nchunk, nq, CHUNK), F32 if exact else jnp.int16),
            pltpu.VMEM((zs, 8, HD), F32),
            pltpu.VMEM((2, zs, 8, HD), F32),
            pltpu.VMEM((4, 8, HD), F32),
            pltpu.VMEM((ys - 1, 8, HD), F32),
            pltpu.VMEM((xcs - 1, 8, HD), F32),
            pltpu.VMEM((zs - 1, 8, HD), F32),
            pltpu.VMEM((8, HD), F32),
            dma((5,)),
            dma((nchunk,)),
            dma((nchunk,)),
            dma((nchunk,)),
            dma,
            dma,
            dma((xcs - 1,)),
            dma((xcs - 1,)),
            dma((zs - 1,)),
            dma((zs - 1,)),
            dma((2, zs)),
            dma((2, zs)),
            dma((ys - 1,)),
            dma((ys - 1,)),
            dma((xcs - 1,)),
            dma((xcs - 1,)),
            dma((zs - 1,)),
            dma((zs - 1,)),
            dma,
            dma,
        ],
        compiler_params=pltpu.CompilerParams(
            collective_id=1 if exact else 0, has_side_effects=True
        ),
    )(hidden, base_kv, delta_codes, block_scales.T, key_gain.reshape(1, HD), queries, kv_cache, lengths)


def split_kernel(both, new_entries, attended):
    new_entries[...] = both[:, :, :HD]
    attended[...] = both[:, :, HD:]


def local(sizes, *args):
    both, narrow = fused(sizes, False, *args)
    both = lax.cond(
        narrow[0] != 0,
        lambda args, fast: fast,
        lambda args, fast: fused(sizes, True, *args)[0],
        args,
        both,
    )
    return pl.pallas_call(
        split_kernel,
        out_shape=(
            jax.ShapeDtypeStruct(both.shape[:2] + (HD,), BF16),
            jax.ShapeDtypeStruct(both.shape[:2] + (both.shape[2] - HD,), BF16),
        ),
    )(both)


def solution(mesh):
    fsdp, tp = mesh.shape["fsdp"], mesh.shape["tp"]
    sizes = (4, fsdp // 4, tp // 2)
    in_specs = (
        P(None, "fsdp", None),
        P(None, "tp"),
        P("fsdp", "tp"),
        P(None, "tp"),
        P(),
        P(None, "fsdp", "tp"),
        P("fsdp", None, "tp"),
        P("fsdp"),
    )
    out_specs = (P(None, "fsdp", "tp"), P(None, "fsdp", "tp"))
    return jax.shard_map(
        functools.partial(local, sizes), mesh=mesh, in_specs=in_specs, out_specs=out_specs, check_vma=False
    )
```
